256 devices in a mesh: seq: 32 (over z, x_hi, core), chan: 8 (over x_lo, y).
Axes of the slice: x: 4 (x_hi: 2, x_lo: 2; x = x_hi * 2 + x_lo), y: 4, z: 8, core: 2. Of those that a mesh axis runs over, the one named last changes fastest.
Arguments:
- features: bfloat16 [8192, 3, 8192], P('seq', None, 'chan'), may hold values from -6 to 6
- residual_in: bfloat16 [8192, 8192], P('seq', 'chan'), may hold values from -6 to 6
- short_filter: float32 [3, 3, 8192], P(None, None, 'chan'), may hold values from -3.5 to 3.5
- decay_rates: float32 [8192, 16], P('chan'), as said below
- residues: float32 [8192, 16], P('chan'), may hold values from -0.12 to 0.12
- skip_gain: float32 [8192], P('chan'), may hold values from -4 to 4
- out_weight: bfloat16 [8192, 8192], P('chan', 'seq'), may hold values from -0.125 to 0.125
- final_gain: float32 [8192], P('chan'), may hold values from 0.5 to 1.5
- embedding: bfloat16 [512, 8192], P(None, 'chan')
- next_ids: int32 [8192], P('seq'), may hold values from 65 to 84, as said below
Outputs:
- block_out: bfloat16 [8192, 8192], P('seq', 'chan')
- log_like: float32 [8192], P('seq')
The draws below stay inside these ranges and needn't reach their ends.
Inputs may be any that keep to these rules, and one draw needn't show every extreme that they name: `next_ids`: each entry is one of 65, 67, 71, 84. `decay_rates`: all between 1.2e-5 and 0.05.
All inputs are finite; a program needn't handle non-finite values.
Results may differ from the reference program's by a relative error of at most 0.015.
Values may be sent and summed in bfloat16 or wider, within the bound.
A program may use at most 128 MiB of HBM per device.

```python
import math
import jax
import jax.numpy as jnp
from jax import lax

D = 8192
VOCAB = 512
SHORT = 3
STATE = 16
TOKENS = 8192


def draw_decay_rates(key, part):
    key = jax.random.fold_in(key, 11)
    lowest = 0.3 / TOKENS
    highest = 0.05
    unit = jax.random.uniform(key, (D, STATE), jnp.float32)
    return jnp.exp(math.log(lowest) + unit * (math.log(highest) - math.log(lowest)))


def draw_embedding(key, part):
    key = jax.random.fold_in(key, 12)
    first_key, second_key = jax.random.split(key, 2)
    scales = jnp.exp(jax.random.uniform(second_key, (VOCAB, 1), jnp.float32) * math.log(1.25))
    basis = jax.random.normal(first_key, (VOCAB, D), jnp.float32) * (3.0 / math.sqrt(D))
    table = basis * scales
    return table.astype(jnp.bfloat16)


def draw_next_ids(key, part):
    key = jax.random.fold_in(key, 13)
    letter = jax.random.randint(key, (TOKENS,), 0, 4)
    alphabet = jnp.array([65, 67, 71, 84], dtype=jnp.int32)
    return alphabet[letter]


def raised(result, key, source, target, parts, factor):
    owner, partner = [(jnp.arange(result.shape[position]) // (result.shape[position] // parts)).reshape([-1 if axis == position else 1 for axis in range(result.ndim)]) for position in (source, target)]
    chosen = jax.random.permutation(key, parts)[partner]
    strong = (owner == chosen) | (owner == (partner + parts // 2) % parts)
    return jnp.where(strong, factor * result, result)


def shard_levels(own_key, dims, shards, least, high):
    factor_of = 1.0
    for axis_at, parts in shards:
        steps = jax.random.uniform(jax.random.fold_in(jax.random.fold_in(own_key, 6), axis_at), (parts,), jnp.float32, least / len(shards), high / len(shards))
        factor_of = factor_of * jnp.repeat(jnp.exp(steps), dims[axis_at] // parts).reshape((-1,) + (1,) * (len(dims) - 1 - axis_at))
    return factor_of


def centred(own_key, extent, scale, limit, shards=(), held_as=jnp.bfloat16):
    entries = scale * jax.random.normal(own_key, extent, jnp.float32)
    if shards:
        entries = entries * shard_levels(own_key, extent, shards, -0.22, 0.18)
    return jnp.clip(entries, -limit, limit).astype(held_as)


def gaussian_with(stream_key, dims, spread, most, cuts, heavy, kind=jnp.bfloat16):
    drawn = spread * jax.random.normal(stream_key, dims, jnp.float32)
    if cuts:
        drawn = drawn * shard_levels(stream_key, dims, cuts, -0.22, 0.18)
    return jnp.clip(raised(drawn, jax.random.fold_in(stream_key, 3), *heavy), -most, most).astype(kind)


def setup_inputs(seed: int = 0) -> dict:
    arg_keys = jax.random.split(jax.random.key(seed), 11)
    return {
        "features": centred(arg_keys[0], (TOKENS, 3, D), 1.0, 6.0, ((0, 32), (2, 8))),
        "residual_in": centred(arg_keys[1], (TOKENS, D), 1.0, 6.0, ((0, 32), (1, 8))),
        "short_filter": centred(arg_keys[2], (SHORT, 3, D), SHORT ** -0.5, 3.5, ((2, 8),), jnp.float32),
        "decay_rates": draw_decay_rates(jax.random.fold_in(arg_keys[10], 71), 0),
        "residues": centred(arg_keys[4], (D, STATE), 0.02, 0.12, ((0, 8),), jnp.float32),
        "skip_gain": centred(arg_keys[5], (D,), 1.0, 4.0, ((0, 8),), jnp.float32),
        "out_weight": gaussian_with(arg_keys[6], (D, D), D ** -0.5, 0.125, ((0, 8), (1, 32)), (0, 1, 32, 2.75)),
        "final_gain": jnp.clip(1.0 + 0.1 * jax.random.normal(arg_keys[7], (D,), jnp.float32), 0.5, 1.5),
        "embedding": draw_embedding(jax.random.fold_in(arg_keys[10], 71), 0),
        "next_ids": draw_next_ids(jax.random.fold_in(arg_keys[10], 71), 0),
    }


def long_block(inputs):
    signal, rates_part, residue_part = inputs
    offsets = jnp.arange(TOKENS, dtype=jnp.float32)
    kernel = jnp.einsum('cm,cmt->ct', residue_part, jnp.exp(-rates_part[:, :, None] * offsets[None, None, :]), precision=lax.Precision.HIGHEST)
    length = 2 * TOKENS
    product = jnp.fft.rfft(signal, n=length) * jnp.fft.rfft(kernel, n=length)
    return jnp.fft.irfft(product, n=length)[:, :TOKENS]

def reference(features, residual_in, short_filter, decay_rates, residues, skip_gain, out_weight, final_gain, embedding, next_ids):
    streams = features.astype(jnp.float32)
    padded = jnp.pad(streams, ((SHORT - 1, 0), (0, 0), (0, 0)))
    short = short_filter[0] * padded[SHORT - 1:SHORT - 1 + TOKENS]
    for offset in range(1, SHORT):
        short = short + short_filter[offset] * padded[SHORT - 1 - offset:SHORT - 1 - offset + TOKENS]
    queries = short[:, 0, :]
    mixed_kv = (short[:, 1, :] * short[:, 2, :]).astype(jnp.bfloat16)
    group_size = min(128, D)
    groups = D // group_size
    signal = mixed_kv.astype(jnp.float32).T.reshape(groups, group_size, TOKENS)
    rates_grouped = decay_rates.reshape(groups, group_size, STATE)
    residue_grouped = residues.reshape(groups, group_size, STATE)
    convolved = lax.map(long_block, (signal, rates_grouped, residue_grouped))
    filtered = convolved.reshape(D, TOKENS).T.astype(jnp.bfloat16)
    gated = (queries * (filtered.astype(jnp.float32) + skip_gain * mixed_kv.astype(jnp.float32))).astype(jnp.bfloat16)
    projected = jnp.dot(gated, out_weight, preferred_element_type=jnp.float32)
    block_out = (residual_in.astype(jnp.float32) + projected).astype(jnp.bfloat16)
    block_f = block_out.astype(jnp.float32)
    inv_rms = lax.rsqrt(lax.optimization_barrier(jnp.mean(block_f * block_f, axis=1)) + 1e-06)
    scaled = (block_f * final_gain).astype(jnp.bfloat16)
    raw_logits = lax.dot_general(scaled, embedding, (((1,), (1,)), ((), ())), preferred_element_type=jnp.float32)
    logits = raw_logits * inv_rms[:, None]
    chosen = jnp.take_along_axis(logits, next_ids[:, None].astype(jnp.int32), axis=1)[:, 0]
    log_like = chosen - jax.nn.logsumexp(logits, axis=1)
    return (block_out, log_like)
```

```python
import functools

import jax
import jax.numpy as jnp
from jax import lax
from jax.experimental import pallas as pl
from jax.experimental.pallas import tpu as pltpu
from jax.sharding import PartitionSpec as P


F32 = jnp.float32
BF16 = jnp.bfloat16
MESH = pl.DeviceIdType.MESH
GROUP = 4
HALO = 2
TAPS = 3
STREAMS = 3
SUB = 8
PAIR = 16


def kernel(
    Z,
    Y,
    x_hbm,
    res_hbm,
    taps_ref,
    rates_ref,
    resid_ref,
    skip_ref,
    w_hbm,
    gain_ref,
    emb_hbm,
    ids_ref,
    bo_hbm,
    ll_ref,
    x_v,
    xf,
    taps,
    rate,
    coef,
    dec1,
    dec_t,
    dec_g,
    halo,
    kv,
    qf,
    g0,
    st,
    p1,
    e_z,
    p2,
    p3_send,
    p3,
    w_all,
    a_all,
    c_send,
    c_recv,
    o_send,
    o_recv,
    res_v,
    emb_v,
    bo_v,
    l_send,
    l_recv,
    s_send,
    s_recv,
    loc_sem,
    halo_sem,
    p1_sem,
    p2_ssem,
    p2_rsem,
    p3_sem,
    sw_sem,
    w_ssem,
    w_rsem,
    sib_ssem,
    sib_rsem,
    a_ssem,
    a_rsem,
    c_ssem,
    c_rsem,
    o_ssem,
    o_rsem,
    l_sem,
    s_sem,
):
    T = x_hbm.shape[1]
    C = x_hbm.shape[2]
    LN = C // SUB
    modes = rates_ref.shape[0]
    MQ = modes // GROUP
    QR = MQ * SUB
    KH = w_hbm.shape[0] // 2
    NB = w_hbm.shape[1]
    SEQ = Z * GROUP
    CHAN = 2 * Y
    NX = 4
    VB = emb_hbm.shape[0] // CHAN
    HT = T // 2

    seq = lax.axis_index("seq")
    chan = lax.axis_index("chan")
    z = seq // 4
    g = seq % 4
    x_hi = g // 2
    core = g % 2
    x_lo = chan // Y
    y = chan % Y
    xx = 2 * x_hi + x_lo

    def dev(zz, gg, cc):
        return {"seq": zz * 4 + gg, "chan": cc}

    def x_dev(xn):
        return dev(z, (xn // 2) * 2 + core, (xn % 2) * Y + y)

    def rcopy(src, dst, ssem, rsem, target):
        return pltpu.make_async_remote_copy(
            src_ref=src, dst_ref=dst, send_sem=ssem, recv_sem=rsem, device_id=target, device_id_type=MESH
        )

    barrier = pltpu.get_barrier_semaphore()
    partners = [dev((z + d) % Z, g, chan) for d in range(1, Z)]
    partners += [dev(z, (g + r) % 4, chan) for r in range(1, 4)]
    partners += [{"seq": (seq + 1) % SEQ, "chan": chan}, {"seq": (seq + SEQ - 1) % SEQ, "chan": chan}]
    partners += [x_dev((xx + r) % NX) for r in range(1, NX)]
    partners += [dev(z, g, (chan + r) % CHAN) for r in range(1, CHAN)]
    swap = dev(z, x_hi * 2 + (1 - core), (1 - x_lo) * Y + y)
    partners += [swap]
    for partner in partners:
        pl.semaphore_signal(barrier, inc=1, device_id=partner, device_id_type=MESH)

    loads = [pltpu.make_async_copy(x_hbm.at[i], x_v.at[i], loc_sem.at[i]) for i in range(STREAMS)]
    load_res = pltpu.make_async_copy(res_hbm, res_v, loc_sem.at[3])
    load_emb = pltpu.make_async_copy(emb_hbm, emb_v, loc_sem.at[4])
    load_w = pltpu.make_async_copy(w_hbm, w_all.at[core, z], loc_sem.at[5])
    native = core == x_lo

    @pl.when(native)
    def _():
        load_w.start()

    for load in loads:
        load.start()
    load_res.start()
    load_emb.start()

    for j in range(SUB):
        lanes = slice(j * LN, (j + 1) * LN)
        rate[pl.ds(j, modes, stride=SUB), :] = rates_ref[:, lanes]
        coef[pl.ds(j, modes, stride=SUB), :] = resid_ref[:, lanes]
        for t in range(TAPS):
            for i in range(STREAMS):
                taps[(t * STREAMS + i) * SUB + j : (t * STREAMS + i) * SUB + j + 1, :] = taps_ref[t, i : i + 1, lanes]
    dec1[...] = jnp.exp(-rate[...])
    dec_t[...] = jnp.exp(-rate[...] * float(T))
    dec_g[...] = jnp.exp(-rate[...] * float(T * GROUP))

    for load in loads:
        load.wait()

    def spread(b):
        rows = pl.ds(pl.multiple_of(b * PAIR, PAIR), PAIR)
        for i in range(STREAMS):
            for j in range(SUB):
                block = x_v[i, rows, j * LN : (j + 1) * LN].astype(F32)
                xf[i, pl.ds(b * PAIR * SUB + j, PAIR, stride=SUB), :] = block

    spread(T // PAIR - 1)
    pl.semaphore_wait(barrier, len(partners))

    halo_copy = rcopy(
        xf.at[:, pl.ds((T - HALO) * SUB, HALO * SUB), :],
        halo,
        halo_sem.at[0],
        halo_sem.at[1],
        {"seq": (seq + 1) % SEQ, "chan": chan},
    )
    halo_copy.start()

    swap_copy = rcopy(w_hbm, w_all.at[x_lo, z], sw_sem.at[0], sw_sem.at[1], swap)

    @pl.when(jnp.logical_not(native))
    def _():
        swap_copy.start()

    up = dev((z + 1) % Z, g, chan)
    down = dev((z + Z - 1) % Z, g, chan)
    sibling = dev(z, x_hi * 2 + (1 - core), chan)
    HALF = Z // 2

    def w_chunk(k, zz, h):
        return w_all.at[k, zz, pl.ds(h * KH, KH), :]

    def ring_copy(flow, d, h):
        if flow == 0:
            zz, target, index = (z + Z - d + 1) % Z, up, 2 * d
        else:
            zz, target, index = (z + d - 1) % Z, down, 2 * d - 1
        if d == HALF:
            index = Z - 1
        ref = w_chunk(core, zz, h)
        return rcopy(ref, ref, w_ssem.at[flow, d - 1, h], w_rsem.at[index, h], target)

    def ring_halves(flow, d):
        return (0, 1) if d < HALF else ((0,) if flow == 0 else (1,))

    def rel(i):
        d = (i + 1) // 2
        return (z + Z + jnp.where(i % 2 == 1, d, -d)) % Z

    def sib_copy(i, h):
        ref = w_chunk(core, rel(i), h)
        return rcopy(ref, ref, sib_ssem.at[i, h], sib_rsem.at[i, h], sibling)

    @pl.when(native)
    def _():
        load_w.wait()

    @pl.when(jnp.logical_not(native))
    def _():
        rcopy(w_hbm, w_all.at[core, z], sw_sem.at[0], sw_sem.at[1], swap).wait_recv()

    for h in range(2):
        for flow in range(2):
            if HALF == 1 and h not in ring_halves(flow, 1):
                continue
            ring_copy(flow, 1, h).start()
    for h in range(2):
        sib_copy(0, h).start()

    def pump(d):
        for h in range(2):
            for flow in range(2):
                if h not in ring_halves(flow, d):
                    continue
                ring_copy(flow, d, h).wait_recv()
                if d < HALF and h in ring_halves(flow, d + 1):
                    ring_copy(flow, d + 1, h).start()
                i = Z - 1 if d == HALF else (2 * d if flow == 0 else 2 * d - 1)
                sib_copy(i, h).start()

    lax.fori_loop(0, T // PAIR - 1, lambda b, c: (spread(b), c)[1], 0)

    halo_copy.wait_recv()
    first = seq == 0

    def tap(t, i):
        return taps[(t * STREAMS + i) * SUB : (t * STREAMS + i + 1) * SUB, :]

    def halo_tile(i, n):
        return jnp.where(first, 0.0, halo[i, n * SUB : (n + 1) * SUB, :])

    def rows_of(t):
        return pl.ds(pl.multiple_of(t * SUB, SUB), SUB)

    def short(i, now, before, before2):
        return tap(0, i) * now + tap(1, i) * before + tap(2, i) * before2

    def mode(ref, m):
        return ref[m * SUB : (m + 1) * SUB, :]

    UN = 4
    zero = jnp.zeros((SUB, LN), F32)

    def state_step(n, carry):
        k1, k2, v1, v2, *s = carry
        for u in range(UN):
            rows = rows_of(n * UN + u)
            k0, v0 = xf[1, rows, :], xf[2, rows, :]
            value = short(1, k0, k1, k2) * short(2, v0, v1, v2)
            kv[rows, :] = value
            s = [mode(dec1, m) * s[m] + value for m in range(modes)]
            k1, k2, v1, v2 = k0, k1, v0, v1
        return (k1, k2, v1, v2, *s)

    last = lax.fori_loop(
        0,
        T // UN,
        state_step,
        (halo_tile(1, 1), halo_tile(1, 0), halo_tile(2, 1), halo_tile(2, 0)) + (zero,) * modes,
    )
    for m in range(modes):
        st[m * SUB : (m + 1) * SUB, :] = last[4 + m]

    def quarter(j):
        return pl.ds(pl.multiple_of(j * QR, QR), QR)

    def p1_copy(r):
        peer = (g + r) % 4
        return rcopy(st.at[quarter(peer), :], p1.at[g], p1_sem.at[0, r - 1], p1_sem.at[1, r - 1], dev(z, peer, chan))

    for r in range(1, 4):
        p1_copy(r).start()
    p1[g] = st[quarter(g), :]

    def local_step(n, carry):
        q1, q2, *s = carry
        for u in range(UN):
            rows = rows_of(n * UN + u)
            q0, value = xf[0, rows, :], kv[rows, :]
            s = [mode(dec1, m) * s[m] + value for m in range(modes)]
            terms = [mode(coef, m) * s[m] for m in range(modes)]
            while len(terms) > 1:
                terms = [terms[2 * n_] + terms[2 * n_ + 1] for n_ in range(len(terms) // 2)]
            qf[rows, :] = short(0, q0, q1, q2)
            g0[rows, :] = terms[0] + skip_ref[...] * value
            q1, q2 = q0, q1
        return (q1, q2, *s)

    for r in range(1, 4):
        p1_copy(r).wait_recv()
    my_t = dec_t[quarter(g), :]
    total = p1[0]
    for j in range(1, 4):
        total = total * my_t + p1[j]
    e_z[...] = total

    def p2_copy(zz, src_z):
        return rcopy(e_z, p2.at[src_z], p2_ssem.at[zz], p2_rsem.at[src_z], dev(zz, g, chan))

    lax.fori_loop(z + 1, Z, lambda zz, c: (p2_copy(zz, z).start(), c)[1], 0)

    lax.fori_loop(0, T // UN, local_step, (halo_tile(0, 1), halo_tile(0, 0)) + (zero,) * modes)

    my_g = dec_g[quarter(g), :]

    def carry_in(zz, c):
        p2_copy(zz, zz).wait_recv()
        return c * my_g + p2[zz]

    enter = lax.fori_loop(0, z, carry_in, jnp.zeros((QR, LN), F32))
    for j in range(4):
        p3_send[j] = enter
        enter = enter * my_t + p1[j]

    def p3_copy(r):
        peer = (g + r) % 4
        return rcopy(p3_send.at[peer], p3.at[quarter(g), :], p3_sem.at[0, r - 1], p3_sem.at[1, r - 1], dev(z, peer, chan))

    for r in range(1, 4):
        p3_copy(r).start()
    p3[quarter(g), :] = p3_send[g]
    pump(1)
    for r in range(1, 4):
        p3_copy(r).wait_recv()

    def gate_step(n, w):
        w = list(w)
        for u in range(UN):
            rows = rows_of(n * UN + u)
            w = [mode(dec1, m) * w[m] for m in range(modes)]
            terms = w
            while len(terms) > 1:
                terms = [terms[2 * n_] + terms[2 * n_ + 1] for n_ in range(len(terms) // 2)]
            g0[rows, :] = qf[rows, :] * (g0[rows, :] + terms[0])
        return tuple(w)

    lax.fori_loop(0, T // UN, gate_step, tuple(mode(coef, m) * mode(p3, m) for m in range(modes)))

    def gather_rows(b, c):
        rows = pl.ds(pl.multiple_of(b * PAIR, PAIR), PAIR)
        for j in range(SUB):
            block = g0[pl.ds(b * PAIR * SUB + j, PAIR, stride=SUB), :]
            a_all[xx, rows, j * LN : (j + 1) * LN] = block.astype(BF16)
        return c

    lax.fori_loop(0, T // PAIR, gather_rows, 0)

    right, left = (xx + 1) % NX, (xx + NX - 1) % NX

    def a_copy(way, block, h, slot):
        ref = a_all.at[block, pl.ds(h * HT, HT), :]
        return rcopy(ref, ref, a_ssem.at[slot, h], a_rsem.at[slot, h], x_dev(right if way == 0 else left))

    for h in range(2):
        a_copy(0, xx, h, 0).start()
        a_copy(1, xx, 1 - h, 1).start()

    pump(2)
    a_copy(0, left, 0, 0).wait_recv()
    a_copy(0, left, 0, 2).start()
    a_copy(1, right, 1, 1).wait_recv()
    a_copy(1, right, 1, 2).start()
    a_copy(0, left, 1, 0).wait_recv()
    a_copy(1, right, 0, 1).wait_recv()

    def c_copy(tb, zz):
        peer, half = zz % Y, zz // Y
        dy = (peer + Y - y) % Y
        return rcopy(
            c_send.at[tb, zz],
            c_recv.at[jnp.maximum(dy - 1, 0), tb, half],
            c_ssem.at[tb, zz],
            c_rsem.at[jnp.maximum(dy - 1, 0), tb, half],
            dev(z, g, x_lo * Y + peer),
        )

    def unit(tb, i):
        zz = rel(i)
        total = jnp.dot(a_all[2 * tb], w_all[0, zz], preferred_element_type=F32)
        total += jnp.dot(a_all[2 * tb + 1], w_all[1, zz], preferred_element_type=F32)
        c_send[tb, zz] = total.astype(BF16)

        @pl.when(zz % Y != y)
        def _():
            c_copy(tb, zz).start()

    def sib_wait(i):
        for h in range(2):
            ref = w_chunk(1 - core, rel(i), h)
            rcopy(ref, ref, sib_ssem.at[i, h], sib_rsem.at[i, h], sibling).wait_recv()

    NEAR = max(Z - 3, 1)

    def near_first(i, c):
        sib_wait(i)
        unit(x_hi, i)
        return c

    def near_second(i, c):
        unit(1 - x_hi, i)
        return c

    def both(i, c):
        sib_wait(i)
        unit(x_hi, i)
        unit(1 - x_hi, i)
        return c

    lax.fori_loop(0, NEAR, near_first, 0)
    for d in range(3, HALF):
        pump(d)
    a_copy(0, (xx + 2) % NX, 0, 2).wait_recv()
    a_copy(1, (xx + 2) % NX, 1, 2).wait_recv()
    lax.fori_loop(0, NEAR, near_second, 0)
    lax.fori_loop(NEAR, Z - 1, both, 0)
    if HALF > 2:
        pump(HALF)
    lax.fori_loop(Z - 1, Z, both, 0)

    def o_copy(tb, half):
        target = 2 * tb + half
        r = (target + NX - xx) % NX
        return rcopy(
            o_send.at[tb, half], o_recv.at[xx], o_ssem.at[tb, half], o_rsem.at[jnp.maximum(r - 1, 0)], x_dev(target)
        )

    def sum_step(n, c):
        tb = (x_hi + n // 2) % 2
        half = n % 2
        total = c_send[tb, half * Y + y].astype(F32)
        for dy in range(1, Y):
            src = c_recv.at[dy - 1, tb, half]
            rcopy(src, src, c_ssem.at[tb, half], c_rsem.at[dy - 1, tb, half], sibling).wait_recv()
            total += c_recv[dy - 1, tb, half].astype(F32)
        value = total.astype(BF16)
        mine = 2 * tb + half == xx

        @pl.when(mine)
        def _():
            o_recv[xx] = value

        @pl.when(jnp.logical_not(mine))
        def _():
            o_send[tb, half] = value
            o_copy(tb, half).start()

        return c

    lax.fori_loop(0, 4, sum_step, 0)
    load_res.wait()
    load_emb.wait()
    for r in range(1, NX):
        src = o_recv.at[(xx + NX - r) % NX]
        rcopy(src, src, o_ssem.at[0, 0], o_rsem.at[r - 1], sibling).wait_recv()

    squares = jnp.zeros((T, LN), F32)
    scaled = []
    for j in range(NX):
        cols = slice(j * NB, (j + 1) * NB)
        value = (res_v[:, cols].astype(F32) + o_recv[j].astype(F32)).astype(BF16)
        bo_v[:, cols] = value
        wide = value.astype(F32)
        for n in range(NB // LN):
            part = wide[:, n * LN : (n + 1) * LN]
            squares += part * part
        scaled.append((wide * gain_ref[:, cols]).astype(BF16))
    store_bo = pltpu.make_async_copy(bo_v, bo_hbm, loc_sem.at[6])
    store_bo.start()

    logits = jnp.zeros((VB * CHAN, T), F32)
    for j in range(NX):
        logits += lax.dot_general(
            emb_v[:, j * NB : (j + 1) * NB], scaled[j], (((1,), (1,)), ((), ())), preferred_element_type=F32
        )
    sums = jnp.sum(squares.T, axis=0, keepdims=True)
    high = sums.astype(BF16)
    low = (sums - high.astype(F32)).astype(BF16)
    row = lax.broadcasted_iota(jnp.int32, (PAIR, T), 0)
    extra = jnp.where(row == 0, high.astype(F32), jnp.where(row == 1, low.astype(F32), 0.0)).astype(BF16)
    for j in range(CHAN):
        l_send[j, :VB, :] = logits[j * VB : (j + 1) * VB, :].astype(BF16)
        l_send[j, VB:, :] = extra

    def l_copy(r):
        peer = (chan + r) % CHAN
        return rcopy(l_send.at[peer], l_recv.at[r - 1], l_sem.at[0, r - 1], l_sem.at[1, r - 1], dev(z, g, peer))

    for r in range(1, CHAN):
        l_copy(r).start()
    full = l_send[chan].astype(F32)
    for r in range(1, CHAN):
        l_copy(r).wait_recv()
        full += l_recv[r - 1].astype(F32)
    mean = (full[VB : VB + 1, :] + full[VB + 1 : VB + 2, :]) / float(C * CHAN)
    scaled_logits = full[:VB, :] * lax.rsqrt(mean + 1e-06)
    vocab = lax.broadcasted_iota(jnp.int32, (VB, T), 0) + chan * VB
    chosen = jnp.sum(jnp.where(vocab == ids_ref[...], scaled_logits, 0.0), axis=0, keepdims=True)
    top = jnp.max(scaled_logits, axis=0, keepdims=True)
    mass = jnp.sum(jnp.exp(scaled_logits - top), axis=0, keepdims=True)
    row = lax.broadcasted_iota(jnp.int32, (SUB, T), 0)
    s_send[...] = jnp.where(row == 0, top, jnp.where(row == 1, mass, jnp.where(row == 2, chosen, 0.0)))

    def s_copy(r):
        return rcopy(
            s_send, s_recv.at[r - 1], s_sem.at[0, r - 1], s_sem.at[1, r - 1], dev(z, g, (chan + r) % CHAN)
        )

    for r in range(1, CHAN):
        s_copy(r).start()
    best = top
    for r in range(1, CHAN):
        s_copy(r).wait_recv()
        best = jnp.maximum(best, s_recv[r - 1, 0:1, :])
    mass = mass * jnp.exp(top - best)
    for r in range(1, CHAN):
        mass += s_recv[r - 1, 1:2, :] * jnp.exp(s_recv[r - 1, 0:1, :] - best)
        chosen += s_recv[r - 1, 2:3, :]
    ll_ref[...] = chosen - best - jnp.log(mass)

    store_bo.wait()
    halo_copy.wait_send()

    @pl.when(jnp.logical_not(native))
    def _():
        swap_copy.wait_send()

    for flow in range(2):
        for d in range(1, HALF + 1):
            for h in ring_halves(flow, d):
                ring_copy(flow, d, h).wait_send()
    for i in range(Z):
        for h in range(2):
            sib_copy(i, h).wait_send()
    for r in range(1, 4):
        p1_copy(r).wait_send()
        p3_copy(r).wait_send()
    lax.fori_loop(z + 1, Z, lambda zz, c: (p2_copy(zz, z).wait_send(), c)[1], 0)
    for h in range(2):
        a_copy(0, xx, h, 0).wait_send()
        a_copy(1, xx, h, 1).wait_send()
    a_copy(0, left, 0, 2).wait_send()
    a_copy(1, right, 1, 2).wait_send()

    def c_done(n, c):
        tb, zz = n // Z, n % Z

        @pl.when(zz % Y != y)
        def _():
            c_copy(tb, zz).wait_send()

        return c

    lax.fori_loop(0, 2 * Z, c_done, 0)

    def o_done(n, c):
        @pl.when(n != xx)
        def _():
            o_copy(n // 2, n % 2).wait_send()

        return c

    lax.fori_loop(0, 4, o_done, 0)
    for r in range(1, CHAN):
        l_copy(r).wait_send()
        s_copy(r).wait_send()


def block(Z, Y, features, residual_in, short_filter, decay_rates, residues, skip_gain, out_weight, final_gain, embedding, next_ids):
    T, _, C = features.shape
    LN = C // SUB
    modes = decay_rates.shape[1]
    QR = modes // GROUP * SUB
    K, NB = out_weight.shape
    V = embedding.shape[0]
    CHAN = 2 * Y
    VB = V // CHAN
    DMA = pltpu.SemaphoreType.DMA
    hbm = pl.BlockSpec(memory_space=pl.ANY)
    vmem = pl.BlockSpec(memory_space=pltpu.VMEM)
    block_out, log_like = pl.pallas_call(
        functools.partial(kernel, Z, Y),
        out_shape=(jax.ShapeDtypeStruct((T, C), BF16), jax.ShapeDtypeStruct((1, T), F32)),
        in_specs=[hbm, hbm, vmem, vmem, vmem, vmem, hbm, vmem, hbm, vmem],
        out_specs=(hbm, vmem),
        scratch_shapes=[
            pltpu.VMEM((STREAMS, T, C), BF16),
            pltpu.VMEM((STREAMS, T * SUB, LN), F32),
            pltpu.VMEM((TAPS * STREAMS * SUB, LN), F32),
            pltpu.VMEM((modes * SUB, LN), F32),
            pltpu.VMEM((modes * SUB, LN), F32),
            pltpu.VMEM((modes * SUB, LN), F32),
            pltpu.VMEM((modes * SUB, LN), F32),
            pltpu.VMEM((modes * SUB, LN), F32),
            pltpu.VMEM((STREAMS, HALO * SUB, LN), F32),
            pltpu.VMEM((T * SUB, LN), F32),
            pltpu.VMEM((T * SUB, LN), F32),
            pltpu.VMEM((T * SUB, LN), F32),
            pltpu.VMEM((modes * SUB, LN), F32),
            pltpu.VMEM((GROUP, QR, LN), F32),
            pltpu.VMEM((QR, LN), F32),
            pltpu.VMEM((Z, QR, LN), F32),
            pltpu.VMEM((GROUP, QR, LN), F32),
            pltpu.VMEM((modes * SUB, LN), F32),
            pltpu.VMEM((2, Z, K, NB), BF16),
            pltpu.VMEM((4, T, C), BF16),
            pltpu.VMEM((2, Z, T, NB), BF16),
            pltpu.VMEM((Y - 1, 2, 2, T, NB), BF16),
            pltpu.VMEM((2, 2, T, NB), BF16),
            pltpu.VMEM((4, T, NB), BF16),
            pltpu.VMEM((T, C), BF16),
            pltpu.VMEM((V, C), BF16),
            pltpu.VMEM((T, C), BF16),
            pltpu.VMEM((CHAN, VB + PAIR, T), BF16),
            pltpu.VMEM((CHAN - 1, VB + PAIR, T), BF16),
            pltpu.VMEM((SUB, T), F32),
            pltpu.VMEM((CHAN - 1, SUB, T), F32),
            DMA((7,)),
            DMA((2,)),
            DMA((2, 3)),
            DMA((Z,)),
            DMA((Z,)),
            DMA((2, 3)),
            DMA((2,)),
            DMA((2, Z // 2, 2)),
            DMA((Z, 2)),
            DMA((Z, 2)),
            DMA((Z, 2)),
            DMA((3, 2)),
            DMA((3, 2)),
            DMA((2, Z)),
            DMA((Y - 1, 2, 2)),
            DMA((2, 2)),
            DMA((3,)),
            DMA((2, CHAN - 1)),
            DMA((2, CHAN - 1)),
        ],
        compiler_params=pltpu.CompilerParams(
            collective_id=0, has_side_effects=True, vmem_limit_bytes=60 * 1024 * 1024
        ),
    )(
        features.transpose(1, 0, 2),
        residual_in,
        short_filter,
        decay_rates.T,
        residues.T,
        skip_gain.reshape(SUB, LN),
        out_weight,
        final_gain.reshape(1, C),
        embedding,
        next_ids.reshape(1, T),
    )
    return block_out, log_like.reshape(T)


def solution(mesh):
    return jax.shard_map(
        functools.partial(block, mesh.shape["seq"] // 4, mesh.shape["chan"] // 2),
        mesh=mesh,
        in_specs=(
            P("seq", None, "chan"),
            P("seq", "chan"),
            P(None, None, "chan"),
            P("chan", None),
            P("chan", None),
            P("chan"),
            P("chan", "seq"),
            P("chan"),
            P(None, "chan"),
            P("seq"),
        ),
        out_specs=(P("seq", "chan"), P("seq")),
        check_vma=False,
    )
```

```python
import functools

import jax
import jax.numpy as jnp
from jax import lax
from jax.experimental import pallas as pl
from jax.experimental.pallas import tpu as pltpu
from jax.sharding import PartitionSpec as P


F32 = jnp.float32
BF16 = jnp.bfloat16
MESH = pl.DeviceIdType.MESH
GROUP = 4
HALO = 2
TAPS = 3
STREAMS = 3
SUB = 8
PAIR = 16


def kernel(
    Z,
    Y,
    x_hbm,
    res_hbm,
    taps_hbm,
    rates_hbm,
    resid_hbm,
    skip_hbm,
    w_hbm,
    gain_hbm,
    emb_hbm,
    ids_hbm,
    bo_hbm,
    ll_ref,
    taps_ref,
    rates_ref,
    resid_ref,
    skip_ref,
    gain_ref,
    ids_ref,
    x_v,
    xf,
    taps,
    rate,
    coef,
    dec1,
    dec_t,
    dec_g,
    halo,
    kv,
    qf,
    g0,
    st,
    p1,
    e_z,
    p2,
    p3_send,
    p3,
    w_all,
    a_all,
    c_send,
    c_relay,
    c_recv,
    o_send,
    o_recv,
    res_v,
    emb_v,
    bo_v,
    l_send,
    l_recv,
    s_send,
    s_recv,
    loc_sem,
    halo_sem,
    p1_sem,
    p2_ssem,
    p2_rsem,
    p3_sem,
    sw_sem,
    w_ssem,
    w_rsem,
    sib_ssem,
    sib_rsem,
    a_ssem,
    a_rsem,
    c_ssem,
    c_rsem,
    r_ssem,
    r_rsem,
    o_ssem,
    o_rsem,
    l_sem,
    s_sem,
):
    T = x_hbm.shape[1]
    C = x_hbm.shape[2]
    LN = C // SUB
    modes = rates_hbm.shape[0]
    MQ = modes // GROUP
    QR = MQ * SUB
    KH = w_hbm.shape[0] // 2
    NB = w_hbm.shape[1]
    SEQ = Z * GROUP
    CHAN = 2 * Y
    NX = 4
    VB = emb_hbm.shape[0] // CHAN
    HT = T // 2
    QS = T // Y // 2

    seq = lax.axis_index("seq")
    chan = lax.axis_index("chan")
    z = seq // 4
    g = seq % 4
    x_hi = g // 2
    core = g % 2
    x_lo = chan // Y
    y = chan % Y
    xx = 2 * x_hi + x_lo

    def dev(zz, gg, cc):
        return {"seq": zz * 4 + gg, "chan": cc}

    def x_dev(xn):
        return dev(z, (xn // 2) * 2 + core, (xn % 2) * Y + y)

    def chip_dev(n):
        xn, yn = n // Y, n % Y
        return dev(z, (xn // 2) * 2 + core, (xn % 2) * Y + yn)

    def rcopy(src, dst, ssem, rsem, target):
        return pltpu.make_async_remote_copy(
            src_ref=src, dst_ref=dst, send_sem=ssem, recv_sem=rsem, device_id=target, device_id_type=MESH
        )

    barrier = pltpu.get_barrier_semaphore()
    partners = [dev((z + d) % Z, g, chan) for d in range(1, Z)]
    partners += [dev(z, (g + r) % 4, chan) for r in range(1, 4)]
    partners += [{"seq": (seq + 1) % SEQ, "chan": chan}, {"seq": (seq + SEQ - 1) % SEQ, "chan": chan}]
    here = xx * Y + y
    partners += [chip_dev((here + r) % (NX * Y)) for r in range(1, NX * Y)]
    swap = dev(z, x_hi * 2 + (1 - core), (1 - x_lo) * Y + y)
    partners += [swap]
    for partner in partners:
        pl.semaphore_signal(barrier, inc=1, device_id=partner, device_id_type=MESH)

    loads = [pltpu.make_async_copy(x_hbm.at[i], x_v.at[i], loc_sem.at[i]) for i in range(STREAMS)]
    load_res = pltpu.make_async_copy(res_hbm, res_v, loc_sem.at[3])
    load_emb = pltpu.make_async_copy(emb_hbm, emb_v, loc_sem.at[4])
    load_w = pltpu.make_async_copy(w_hbm, w_all.at[core, z], loc_sem.at[5])
    smalls = [
        pltpu.make_async_copy(src, dst, loc_sem.at[7 + n])
        for n, (src, dst) in enumerate(
            (
                (rates_hbm, rates_ref),
                (resid_hbm, resid_ref),
                (taps_hbm, taps_ref),
                (skip_hbm, skip_ref),
                (gain_hbm, gain_ref),
                (ids_hbm, ids_ref),
            )
        )
    ]
    native = core == x_lo

    @pl.when(native)
    def _():
        load_w.start()

    for load in smalls + loads:
        load.start()
    load_res.start()
    load_emb.start()

    for load in smalls:
        load.wait()
    for j in range(SUB):
        lanes = slice(j * LN, (j + 1) * LN)
        rate[pl.ds(j, modes, stride=SUB), :] = rates_ref[:, lanes]
        coef[pl.ds(j, modes, stride=SUB), :] = resid_ref[:, lanes]
        for t in range(TAPS):
            for i in range(STREAMS):
                taps[(t * STREAMS + i) * SUB + j : (t * STREAMS + i) * SUB + j + 1, :] = taps_ref[t, i : i + 1, lanes]
    dec1[...] = jnp.exp(-rate[...])
    dec_t[...] = jnp.exp(-rate[...] * float(T))
    dec_g[...] = jnp.exp(-rate[...] * float(T * GROUP))

    for load in loads:
        load.wait()

    def spread(b):
        rows = pl.ds(pl.multiple_of(b * PAIR, PAIR), PAIR)
        for i in range(STREAMS):
            for j in range(SUB):
                block = x_v[i, rows, j * LN : (j + 1) * LN].astype(F32)
                xf[i, pl.ds(b * PAIR * SUB + j, PAIR, stride=SUB), :] = block

    lax.fori_loop(0, T // PAIR, lambda b, c: (spread(b), c)[1], 0)

    def tap(t, i):
        return taps[(t * STREAMS + i) * SUB : (t * STREAMS + i + 1) * SUB, :]

    def rows_of(t):
        return pl.ds(pl.multiple_of(t * SUB, SUB), SUB)

    def short(i, now, before, before2):
        return tap(0, i) * now + tap(1, i) * before + tap(2, i) * before2

    def mode(ref, m):
        return ref[m * SUB : (m + 1) * SUB, :]

    UN = 4
    zero = jnp.zeros((SUB, LN), F32)

    def state_one(rows, carry):
        k1, k2, v1, v2, *s = carry
        k0, v0 = xf[1, rows, :], xf[2, rows, :]
        value = short(1, k0, k1, k2) * short(2, v0, v1, v2)
        kv[rows, :] = value
        s = [mode(dec1, m) * s[m] + value for m in range(modes)]
        return (k0, k1, v0, v1, *s)

    def state_step(n, carry):
        for u in range(UN):
            carry = state_one(rows_of(n * UN + u), carry)
        return carry

    def at(i, t):
        return xf[i, t * SUB : (t + 1) * SUB, :]

    last = (at(1, 1), at(1, 0), at(2, 1), at(2, 0)) + (zero,) * modes
    for t in range(HALO, UN):
        last = state_one(rows_of(t), last)
    last = lax.fori_loop(
        1,
        T // UN,
        state_step,
        last,
    )
    for m in range(modes):
        st[m * SUB : (m + 1) * SUB, :] = last[4 + m]
    dec_a = jnp.exp(-rate[...] * float(T - 2))

    pl.semaphore_wait(barrier, len(partners))

    def halo_(): return rcopy(
        xf.at[:, pl.ds((T - HALO) * SUB, HALO * SUB), :],
        halo,
        halo_sem.at[0],
        halo_sem.at[1],
        {"seq": (seq + 1) % SEQ, "chan": chan},
    )
    halo_copy = halo_()
    halo_copy.start()

    def swap_(): return rcopy(w_hbm, w_all.at[x_lo, z], sw_sem.at[0], sw_sem.at[1], swap)

    swap_copy = swap_()
    @pl.when(jnp.logical_not(native))
    def _():
        swap_copy.start()

    up = dev((z + 1) % Z, g, chan)
    down = dev((z + Z - 1) % Z, g, chan)
    sibling = dev(z, x_hi * 2 + (1 - core), chan)
    HALF = Z // 2

    def w_chunk(k, zz, h):
        return w_all.at[k, zz, pl.ds(h * KH, KH), :]

    def ring_copy(flow, d, h):
        if flow == 0:
            zz, target, index = (z + Z - d + 1) % Z, up, 2 * d
        else:
            zz, target, index = (z + d - 1) % Z, down, 2 * d - 1
        if d == HALF:
            index = Z - 1
        ref = w_chunk(core, zz, h)
        return rcopy(ref, ref, w_ssem.at[flow, d - 1, h], w_rsem.at[index, h], target)

    def ring_halves(flow, d):
        return (0, 1) if d < HALF else ((0,) if flow == 0 else (1,))

    def rel(i):
        d = (i + 1) // 2
        return (z + Z + jnp.where(i % 2 == 1, d, -d)) % Z

    def sib_copy(i, h):
        ref = w_chunk(core, rel(i), h)
        return rcopy(ref, ref, sib_ssem.at[i, h], sib_rsem.at[i, h], sibling)

    def ring_first():
        for flow in range(2):
            ring_copy(flow, 1, 0).start()
        for h in range(2):
            sib_copy(0, h).start()

    def ring_second():
        for flow in range(2):
            ring_copy(flow, 1, 0).wait_send()
        for flow in range(2):
            ring_copy(flow, 1, 1).start()

    @pl.when(native)
    def _():
        load_w.wait()
        ring_first()
        ring_second()

    def pump(d, h):
        for flow in range(2):
            if h not in ring_halves(flow, d):
                continue
            ring_copy(flow, d, h).wait_recv()
            if d < HALF and h in ring_halves(flow, d + 1):
                ring_copy(flow, d + 1, h).start()
            i = Z - 1 if d == HALF else (2 * d if flow == 0 else 2 * d - 1)
            sib_copy(i, h).start()

    def other_start():
        @pl.when(jnp.logical_not(native))
        def _():
            swap_().wait_recv()
            ring_first()

    def pumps(cond, *steps):
        @pl.when(cond)
        def _():
            for d, h in steps:
                pump(d, h)

    other = jnp.logical_not(native)

    halo_copy.wait_recv()
    first = seq == 0

    def halo_tile(i, n):
        return jnp.where(first, 0.0, halo[i, n * SUB : (n + 1) * SUB, :])

    heads = []
    for t in range(HALO):
        pair = []
        for i in (1, 2):
            seen = [halo_tile(i, 0), halo_tile(i, 1), at(i, 0), at(i, 1)]
            pair.append(short(i, seen[t + 2], seen[t + 1], seen[t]))
        heads.append(pair[0] * pair[1])
        kv[t * SUB : (t + 1) * SUB, :] = heads[t]
    for m in range(modes):
        rows = slice(m * SUB, (m + 1) * SUB)
        st[rows, :] += dec_a[rows, :] * (mode(dec1, m) * heads[0] + heads[1])

    def quarter(j):
        return pl.ds(pl.multiple_of(j * QR, QR), QR)

    def p1_copy(r):
        peer = (g + r) % 4
        return rcopy(st.at[quarter(peer), :], p1.at[g], p1_sem.at[0, r - 1], p1_sem.at[1, r - 1], dev(z, peer, chan))

    for r in range(1, 4):
        p1_copy(r).start()
    p1[g] = st[quarter(g), :]

    def local_step(n, carry):
        q1, q2, *s = carry
        for u in range(UN):
            rows = rows_of(n * UN + u)
            q0, value = xf[0, rows, :], kv[rows, :]
            s = [mode(dec1, m) * s[m] + value for m in range(modes)]
            terms = [mode(coef, m) * s[m] for m in range(modes)]
            while len(terms) > 1:
                terms = [terms[2 * n_] + terms[2 * n_ + 1] for n_ in range(len(terms) // 2)]
            qf[rows, :] = short(0, q0, q1, q2)
            g0[rows, :] = terms[0] + skip_ref[...] * value
            q1, q2 = q0, q1
        return (q1, q2, *s)

    pumps(native, (1, 0))
    half_way = lax.fori_loop(0, T // UN // 2, local_step, (halo_tile(0, 1), halo_tile(0, 0)) + (zero,) * modes)
    for r in range(1, 4):
        p1_copy(r).wait_recv()
    my_t = dec_t[quarter(g), :]
    total = p1[0]
    for j in range(1, 4):
        total = total * my_t + p1[j]
    e_z[...] = total

    def p2_copy(zz, src_z):
        return rcopy(e_z, p2.at[src_z], p2_ssem.at[zz], p2_rsem.at[src_z], dev(zz, g, chan))

    lax.fori_loop(z + 1, Z, lambda zz, c: (p2_copy(zz, z).start(), c)[1], 0)

    other_start()
    pumps(native, (1, 1))
    lax.fori_loop(T // UN // 2, T // UN, local_step, half_way)
    pumps(native, (2, 0))

    my_g = dec_g[quarter(g), :]

    def carry_in(zz, c):
        p2_copy(zz, zz).wait_recv()
        return c * my_g + p2[zz]

    enter = lax.fori_loop(0, z, carry_in, jnp.zeros((QR, LN), F32))
    for j in range(4):
        p3_send[j] = enter
        enter = enter * my_t + p1[j]

    def p3_copy(r):
        peer = (g + r) % 4
        return rcopy(p3_send.at[peer], p3.at[quarter(g), :], p3_sem.at[0, r - 1], p3_sem.at[1, r - 1], dev(z, peer, chan))

    for r in range(1, 4):
        p3_copy(r).start()
    p3[quarter(g), :] = p3_send[g]

    @pl.when(other)
    def _():
        ring_second()

    pumps(native, (2, 1))
    pumps(other, (1, 0))
    for r in range(1, 4):
        p3_copy(r).wait_recv()

    def gate_step(n, w):
        w = list(w)
        for u in range(UN):
            rows = rows_of(n * UN + u)
            w = [mode(dec1, m) * w[m] for m in range(modes)]
            terms = w
            while len(terms) > 1:
                terms = [terms[2 * n_] + terms[2 * n_ + 1] for n_ in range(len(terms) // 2)]
            g0[rows, :] = qf[rows, :] * (g0[rows, :] + terms[0])
        return tuple(w)

    lax.fori_loop(0, T // UN, gate_step, tuple(mode(coef, m) * mode(p3, m) for m in range(modes)))

    def gather_rows(b, c):
        rows = pl.ds(pl.multiple_of(b * PAIR, PAIR), PAIR)
        for j in range(SUB):
            block = g0[pl.ds(b * PAIR * SUB + j, PAIR, stride=SUB), :]
            a_all[xx, rows, j * LN : (j + 1) * LN] = block.astype(BF16)
        return c

    lax.fori_loop(0, T // PAIR, gather_rows, 0)

    right, left = (xx + 1) % NX, (xx + NX - 1) % NX

    def a_copy(way, h, relay):
        rows = pl.ds(h * HT + (way * HT // 2 if relay else 0), HT // 2 if relay else HT)
        return rows, way + 2 * relay, x_dev(right if way == 0 else left)

    def a_out(way, h, relay=0):
        rows, slot, target = a_copy(way, h, relay)
        ref = a_all.at[(left if way == 0 else right) if relay else xx, rows, :]
        return rcopy(ref, ref, a_ssem.at[slot, h], a_rsem.at[slot, h], target)

    def a_in(way, h, relay=0):
        rows, slot, target = a_copy(way, h, relay)
        ref = a_all.at[(xx + 2) % NX if relay else (left if way == 0 else right), rows, :]
        return rcopy(ref, ref, a_ssem.at[slot, h], a_rsem.at[slot, h], target)

    def a_pass(h):
        for way in range(2):
            a_in(way, h).wait_recv()
            a_out(way, h, 1).start()

    def a_far(h):
        for way in range(2):
            a_in(way, h, 1).wait_recv()

    for way in range(2):
        a_out(way, 0).start()
    pumps(native, (3, 0))
    pumps(other, (1, 1))
    for way in range(2):
        a_out(way, 0).wait_send()
        a_out(way, 1).start()
    pumps(native, (3, 1))
    pumps(other, (2, 0))

    GROUPS = ((0, 3), (3, 5), (5, 7), (7, 8))

    def span(n):
        return pl.ds(GROUPS[n][0], GROUPS[n][1] - GROUPS[n][0])

    def y_next(way):
        return (y + 1) % Y if way == 0 else (y + Y - 1) % Y

    def r_copy(tb, n, way):
        return rcopy(
            c_send.at[tb, (y + 2) % Y, span(n), way],
            c_relay.at[way, tb, span(n)],
            r_ssem.at[way, tb, n],
            r_rsem.at[way, tb, n],
            dev(z, g, x_lo * Y + y_next(way)),
        )

    def c_copy(tb, n, way):
        return rcopy(
            c_send.at[tb, y_next(way), span(n)],
            c_recv.at[way, tb, span(n)],
            c_ssem.at[way, tb, n],
            c_rsem.at[way, tb, n],
            dev(z, g, x_lo * Y + y_next(way)),
        )

    def relay(tb, n):
        for way in range(2):
            r_copy(tb, n, way).wait_recv()
            peer = y_next(way)

            def step(i, c):
                mine = c_send[tb, peer, i, way].astype(F32)
                c_send[tb, peer, i, way] = (mine + c_relay[way, tb, i].astype(F32)).astype(BF16)
                return c

            lax.fori_loop(GROUPS[n][0], GROUPS[n][1], step, 0)
            c_copy(tb, n, way).start()

    def sib_wait(i):
        for h in range(2):
            ref = w_chunk(1 - core, rel(i), h)
            rcopy(ref, ref, sib_ssem.at[i, h], sib_rsem.at[i, h], sibling).wait_recv()

    def unit(tb, i, halves):
        zz = rel(i)
        rows = pl.ds(halves[0] * HT, len(halves) * HT)
        total = jnp.dot(a_all[2 * tb, rows, :], w_all[0, zz], preferred_element_type=F32)
        total += jnp.dot(a_all[2 * tb + 1, rows, :], w_all[1, zz], preferred_element_type=F32)
        value = total.astype(BF16)
        for at_, h in enumerate(halves):
            for n in range(Y):
                c_send[tb, n, i, h] = value[at_ * HT + n * QS : at_ * HT + (n + 1) * QS, :]

    def units(tb, n, halves, fresh=False):
        def step(i, c):
            if fresh:
                sib_wait(i)
            unit(tb, i, halves)
            return c

        lax.fori_loop(GROUPS[n][0], GROUPS[n][1], step, 0)
        for way in range(2):
            r_copy(tb, n, way).start()

    def o_copy(tb, i):
        zz = rel(i)
        return rcopy(
            o_send.at[tb, i],
            o_recv.at[xx, :, y],
            o_ssem.at[tb, i],
            o_rsem.at[here],
            dev(z, tb * 2 + core, zz),
        )

    def is_mine(tb, i):
        return jnp.logical_and(tb == x_hi, rel(i) == chan)

    def sum_group(tb, n):
        for way in range(2):
            c_copy(tb, n, way).wait_recv()

        def step(i, c):
            total = c_send[tb, y, i].astype(F32)
            for way in range(2):
                total += c_recv[way, tb, i].astype(F32)
            value = total.astype(BF16)

            @pl.when(is_mine(tb, i))
            def _():
                o_recv[xx, :, y] = value

            @pl.when(jnp.logical_not(is_mine(tb, i)))
            def _():
                o_send[tb, i] = value
                o_copy(tb, i).start()

            return c

        lax.fori_loop(GROUPS[n][0], GROUPS[n][1], step, 0)

    near, far = x_hi, 1 - x_hi
    whole = (0, 1)
    a_pass(0)
    pumps(other, (2, 1))
    a_pass(1)
    units(near, 0, whole, True)
    pumps(other, (3, 0))
    units(near, 1, whole, True)
    pumps(other, (3, 1))
    relay(near, 0)
    pumps(native, (4, 0), (4, 1))
    a_far(0)
    a_far(1)
    units(far, 0, whole)
    relay(near, 1)
    units(far, 1, whole)
    units(near, 2, whole, True)
    relay(far, 0)
    units(far, 2, whole)
    relay(far, 1)
    relay(near, 2)
    relay(far, 2)
    pumps(other, (4, 0), (4, 1))
    units(near, 3, whole, True)
    units(far, 3, whole)

    sum_group(near, 0)
    sum_group(near, 1)
    relay(near, 3)
    relay(far, 3)
    sum_group(far, 0)
    sum_group(far, 1)
    sum_group(near, 2)
    sum_group(far, 2)
    sum_group(near, 3)
    sum_group(far, 3)
    load_res.wait()
    load_emb.wait()

    def o_in(n):
        ref = o_recv.at[n // Y, :, n % Y]
        return rcopy(ref, ref, o_ssem.at[0, 0], o_rsem.at[n], sibling)

    def o_wait(n, c):
        @pl.when(n != here)
        def _():
            o_in(n).wait_recv()

        return c

    lax.fori_loop(0, NX * Y, o_wait, 0)

    squares = jnp.zeros((T, LN), F32)
    scaled = []
    for j in range(NX):
        cols = slice(j * NB, (j + 1) * NB)
        value = (res_v[:, cols].astype(F32) + o_recv[j].reshape(T, NB).astype(F32)).astype(BF16)
        bo_v[:, cols] = value
        wide = value.astype(F32)
        for n in range(NB // LN):
            part = wide[:, n * LN : (n + 1) * LN]
            squares += part * part
        scaled.append((wide * gain_ref[:, cols]).astype(BF16))
    store_bo = pltpu.make_async_copy(bo_v, bo_hbm, loc_sem.at[6])
    store_bo.start()

    logits = jnp.zeros((VB * CHAN, T), F32)
    for j in range(NX):
        logits += lax.dot_general(
            emb_v[:, j * NB : (j + 1) * NB], scaled[j], (((1,), (1,)), ((), ())), preferred_element_type=F32
        )
    sums = jnp.sum(squares.T, axis=0, keepdims=True)
    high = sums.astype(BF16)
    low = (sums - high.astype(F32)).astype(BF16)
    row = lax.broadcasted_iota(jnp.int32, (PAIR, T), 0)
    extra = jnp.where(row == 0, high.astype(F32), jnp.where(row == 1, low.astype(F32), 0.0)).astype(BF16)
    for j in range(CHAN):
        l_send[j, :VB, :] = logits[j * VB : (j + 1) * VB, :].astype(BF16)
        l_send[j, VB:, :] = extra

    def l_copy(r):
        peer = (chan + r) % CHAN
        return rcopy(l_send.at[peer], l_recv.at[r - 1], l_sem.at[0, r - 1], l_sem.at[1, r - 1], dev(z, g, peer))

    for r in range(1, CHAN):
        l_copy(r).start()
    full = l_send[chan].astype(F32)
    for r in range(1, CHAN):
        l_copy(r).wait_recv()
        full += l_recv[r - 1].astype(F32)
    mean = (full[VB : VB + 1, :] + full[VB + 1 : VB + 2, :]) / float(C * CHAN)
    scaled_logits = full[:VB, :] * lax.rsqrt(mean + 1e-06)
    vocab = lax.broadcasted_iota(jnp.int32, (VB, T), 0) + chan * VB
    chosen = jnp.sum(jnp.where(vocab == ids_ref[...], scaled_logits, 0.0), axis=0, keepdims=True)
    top = jnp.max(scaled_logits, axis=0, keepdims=True)
    mass = jnp.sum(jnp.exp(scaled_logits - top), axis=0, keepdims=True)
    row = lax.broadcasted_iota(jnp.int32, (SUB, T), 0)
    s_send[...] = jnp.where(row == 0, top, jnp.where(row == 1, mass, jnp.where(row == 2, chosen, 0.0)))

    def s_copy(r):
        return rcopy(
            s_send, s_recv.at[r - 1], s_sem.at[0, r - 1], s_sem.at[1, r - 1], dev(z, g, (chan + r) % CHAN)
        )

    for r in range(1, CHAN):
        s_copy(r).start()
    best = top
    for r in range(1, CHAN):
        s_copy(r).wait_recv()
        best = jnp.maximum(best, s_recv[r - 1, 0:1, :])
    mass = mass * jnp.exp(top - best)
    for r in range(1, CHAN):
        mass += s_recv[r - 1, 1:2, :] * jnp.exp(s_recv[r - 1, 0:1, :] - best)
        chosen += s_recv[r - 1, 2:3, :]
    ll_ref[...] = chosen - best - jnp.log(mass)

    store_bo.wait()
    halo_copy.wait_send()

    @pl.when(jnp.logical_not(native))
    def _():
        swap_copy.wait_send()

    for flow in range(2):
        for d in range(1, HALF + 1):
            for h in ring_halves(flow, d):
                if (d, h) != (1, 0):
                    ring_copy(flow, d, h).wait_send()
    for i in range(Z):
        for h in range(2):
            sib_copy(i, h).wait_send()
    for r in range(1, 4):
        p1_copy(r).wait_send()
        p3_copy(r).wait_send()
    lax.fori_loop(z + 1, Z, lambda zz, c: (p2_copy(zz, z).wait_send(), c)[1], 0)
    for way in range(2):
        a_out(way, 1).wait_send()
        for h in range(2):
            a_out(way, h, 1).wait_send()
    for tb in range(2):
        for n in range(len(GROUPS)):
            for way in range(2):
                r_copy(tb, n, way).wait_send()
                c_copy(tb, n, way).wait_send()

    def o_done(n, c):
        tb, i = n // Z, n % Z

        @pl.when(jnp.logical_not(is_mine(tb, i)))
        def _():
            o_copy(tb, i).wait_send()

        return c

    lax.fori_loop(0, 2 * Z, o_done, 0)
    for r in range(1, CHAN):
        l_copy(r).wait_send()
        s_copy(r).wait_send()


def block(Z, Y, features, residual_in, short_filter, decay_rates, residues, skip_gain, out_weight, final_gain, embedding, next_ids):
    T, _, C = features.shape
    LN = C // SUB
    modes = decay_rates.shape[1]
    QR = modes // GROUP * SUB
    K, NB = out_weight.shape
    V = embedding.shape[0]
    CHAN = 2 * Y
    VB = V // CHAN
    QS = T // Y // 2
    DMA = pltpu.SemaphoreType.DMA
    hbm = pl.BlockSpec(memory_space=pl.ANY)
    vmem = pl.BlockSpec(memory_space=pltpu.VMEM)
    block_out, log_like = pl.pallas_call(
        functools.partial(kernel, Z, Y),
        out_shape=(jax.ShapeDtypeStruct((T, C), BF16), jax.ShapeDtypeStruct((1, T), F32)),
        in_specs=[hbm] * 10,
        out_specs=(hbm, vmem),
        scratch_shapes=[
            pltpu.VMEM((TAPS, STREAMS, C), F32),
            pltpu.VMEM((modes, C), F32),
            pltpu.VMEM((modes, C), F32),
            pltpu.VMEM((SUB, LN), F32),
            pltpu.VMEM((1, C), F32),
            pltpu.VMEM((1, T), jnp.int32),
            pltpu.VMEM((STREAMS, T, C), BF16),
            pltpu.VMEM((STREAMS, T * SUB, LN), F32),
            pltpu.VMEM((TAPS * STREAMS * SUB, LN), F32),
            pltpu.VMEM((modes * SUB, LN), F32),
            pltpu.VMEM((modes * SUB, LN), F32),
            pltpu.VMEM((modes * SUB, LN), F32),
            pltpu.VMEM((modes * SUB, LN), F32),
            pltpu.VMEM((modes * SUB, LN), F32),
            pltpu.VMEM((STREAMS, HALO * SUB, LN), F32),
            pltpu.VMEM((T * SUB, LN), F32),
            pltpu.VMEM((T * SUB, LN), F32),
            pltpu.VMEM((T * SUB, LN), F32),
            pltpu.VMEM((modes * SUB, LN), F32),
            pltpu.VMEM((GROUP, QR, LN), F32),
            pltpu.VMEM((QR, LN), F32),
            pltpu.VMEM((Z, QR, LN), F32),
            pltpu.VMEM((GROUP, QR, LN), F32),
            pltpu.VMEM((modes * SUB, LN), F32),
            pltpu.VMEM((2, Z, K, NB), BF16),
            pltpu.VMEM((4, T, C), BF16),
            pltpu.VMEM((2, Y, Z, 2, QS, NB), BF16),
            pltpu.VMEM((2, 2, Z, QS, NB), BF16),
            pltpu.VMEM((2, 2, Z, 2, QS, NB), BF16),
            pltpu.VMEM((2, Z, 2, QS, NB), BF16),
            pltpu.VMEM((4, 2, Y, QS, NB), BF16),
            pltpu.VMEM((T, C), BF16),
            pltpu.VMEM((V, C), BF16),
            pltpu.VMEM((T, C), BF16),
            pltpu.VMEM((CHAN, VB + PAIR, T), BF16),
            pltpu.VMEM((CHAN - 1, VB + PAIR, T), BF16),
            pltpu.VMEM((SUB, T), F32),
            pltpu.VMEM((CHAN - 1, SUB, T), F32),
            DMA((13,)),
            DMA((2,)),
            DMA((2, 3)),
            DMA((Z,)),
            DMA((Z,)),
            DMA((2, 3)),
            DMA((2,)),
            DMA((2, Z // 2, 2)),
            DMA((Z, 2)),
            DMA((Z, 2)),
            DMA((Z, 2)),
            DMA((4, 2)),
            DMA((4, 2)),
            DMA((2, 2, 4)),
            DMA((2, 2, 4)),
            DMA((2, 2, 4)),
            DMA((2, 2, 4)),
            DMA((2, Z)),
            DMA((4 * Y,)),
            DMA((2, CHAN - 1)),
            DMA((2, CHAN - 1)),
        ],
        compiler_params=pltpu.CompilerParams(
            collective_id=0, has_side_effects=True, vmem_limit_bytes=60 * 1024 * 1024
        ),
    )(
        features.transpose(1, 0, 2),
        residual_in,
        short_filter,
        decay_rates.T,
        residues.T,
        skip_gain.reshape(SUB, LN),
        out_weight,
        final_gain.reshape(1, C),
        embedding,
        next_ids.reshape(1, T),
    )
    return block_out, log_like.reshape(T)


def solution(mesh):
    return jax.shard_map(
        functools.partial(block, mesh.shape["seq"] // 4, mesh.shape["chan"] // 2),
        mesh=mesh,
        in_specs=(
            P("seq", None, "chan"),
            P("seq", "chan"),
            P(None, None, "chan"),
            P("chan", None),
            P("chan", None),
            P("chan"),
            P("chan", "seq"),
            P("chan"),
            P(None, "chan"),
            P("seq"),
        ),
        out_specs=(P("seq", "chan"), P("seq")),
        check_vma=False,
    )
```

```python
import functools

import jax
import jax.numpy as jnp
from jax import lax
from jax.experimental import pallas as pl
from jax.experimental.pallas import tpu as pltpu
from jax.sharding import PartitionSpec as P


F32 = jnp.float32
BF16 = jnp.bfloat16
MESH = pl.DeviceIdType.MESH
GROUP = 4
HALO = 2
TAPS = 3
STREAMS = 3
SUB = 8
PAIR = 16


def kernel(
    Z,
    Y,
    x_hbm,
    res_hbm,
    taps_hbm,
    rates_hbm,
    resid_hbm,
    skip_hbm,
    w_hbm,
    gain_hbm,
    emb_hbm,
    ids_hbm,
    bo_hbm,
    ll_ref,
    taps_ref,
    rates_ref,
    resid_ref,
    skip_ref,
    gain_ref,
    ids_ref,
    x_v,
    xf,
    taps,
    rate,
    coef,
    dec1,
    dec_t,
    dec_g,
    halo,
    kv,
    qf,
    g0,
    st,
    p1,
    e_z,
    p2,
    p3_send,
    p3,
    w_all,
    a_all,
    c_send,
    c_relay,
    c_recv,
    o_send,
    o_recv,
    res_v,
    emb_v,
    bo_v,
    l_send,
    l_recv,
    s_send,
    s_recv,
    loc_sem,
    halo_sem,
    p1_sem,
    p2_ssem,
    p2_rsem,
    p3_sem,
    sw_sem,
    w_ssem,
    w_rsem,
    sib_ssem,
    sib_rsem,
    a_ssem,
    a_rsem,
    c_ssem,
    c_rsem,
    r_ssem,
    r_rsem,
    o_ssem,
    o_rsem,
    l_sem,
    s_sem,
):
    T = x_hbm.shape[1]
    C = x_hbm.shape[2]
    LN = C // SUB
    modes = rates_hbm.shape[0]
    MQ = modes // GROUP
    QR = MQ * SUB
    KH = w_hbm.shape[0] // 2
    NB = w_hbm.shape[1]
    SEQ = Z * GROUP
    CHAN = 2 * Y
    NX = 4
    VB = emb_hbm.shape[0] // CHAN
    HT = T // 2
    QS = T // Y // 2

    seq = lax.axis_index("seq")
    chan = lax.axis_index("chan")
    z = seq // 4
    g = seq % 4
    x_hi = g // 2
    core = g % 2
    x_lo = chan // Y
    y = chan % Y
    xx = 2 * x_hi + x_lo

    def dev(zz, gg, cc):
        return {"seq": zz * 4 + gg, "chan": cc}

    def x_dev(xn):
        return dev(z, (xn // 2) * 2 + core, (xn % 2) * Y + y)

    def chip_dev(n):
        xn, yn = n // Y, n % Y
        return dev(z, (xn // 2) * 2 + core, (xn % 2) * Y + yn)

    def rcopy(src, dst, ssem, rsem, target):
        return pltpu.make_async_remote_copy(
            src_ref=src, dst_ref=dst, send_sem=ssem, recv_sem=rsem, device_id=target, device_id_type=MESH
        )

    barrier = pltpu.get_barrier_semaphore()
    partners = [dev((z + d) % Z, g, chan) for d in range(1, Z)]
    partners += [dev(z, (g + r) % 4, chan) for r in range(1, 4)]
    partners += [{"seq": (seq + 1) % SEQ, "chan": chan}, {"seq": (seq + SEQ - 1) % SEQ, "chan": chan}]
    here = xx * Y + y
    partners += [chip_dev((here + r) % (NX * Y)) for r in range(1, NX * Y)]
    swap = dev(z, x_hi * 2 + (1 - core), (1 - x_lo) * Y + y)
    partners += [swap]
    for partner in partners:
        pl.semaphore_signal(barrier, inc=1, device_id=partner, device_id_type=MESH)

    loads = [pltpu.make_async_copy(x_hbm.at[i], x_v.at[i], loc_sem.at[i]) for i in range(STREAMS)]
    load_res = pltpu.make_async_copy(res_hbm, res_v, loc_sem.at[3])
    load_emb = pltpu.make_async_copy(emb_hbm, emb_v, loc_sem.at[4])
    load_w = pltpu.make_async_copy(w_hbm, w_all.at[core, z], loc_sem.at[5])
    smalls = [
        pltpu.make_async_copy(src, dst, loc_sem.at[7 + n])
        for n, (src, dst) in enumerate(
            (
                (rates_hbm, rates_ref),
                (resid_hbm, resid_ref),
                (taps_hbm, taps_ref),
                (skip_hbm, skip_ref),
                (gain_hbm, gain_ref),
                (ids_hbm, ids_ref),
            )
        )
    ]
    native = core == x_lo

    @pl.when(native)
    def _():
        load_w.start()

    for load in smalls + loads:
        load.start()
    load_res.start()
    load_emb.start()

    for load in smalls:
        load.wait()
    for j in range(SUB):
        lanes = slice(j * LN, (j + 1) * LN)
        rate[pl.ds(j, modes, stride=SUB), :] = rates_ref[:, lanes]
        coef[pl.ds(j, modes, stride=SUB), :] = resid_ref[:, lanes]
        for t in range(TAPS):
            for i in range(STREAMS):
                taps[(t * STREAMS + i) * SUB + j : (t * STREAMS + i) * SUB + j + 1, :] = taps_ref[t, i : i + 1, lanes]
    dec1[...] = jnp.exp(-rate[...])
    dec_t[...] = jnp.exp(-rate[...] * float(T))
    dec_g[...] = jnp.exp(-rate[...] * float(T * GROUP))

    for load in loads:
        load.wait()

    def spread(b):
        rows = pl.ds(pl.multiple_of(b * PAIR, PAIR), PAIR)
        for i in range(STREAMS):
            for j in range(SUB):
                block = x_v[i, rows, j * LN : (j + 1) * LN].astype(F32)
                xf[i, pl.ds(b * PAIR * SUB + j, PAIR, stride=SUB), :] = block

    lax.fori_loop(0, T // PAIR, lambda b, c: (spread(b), c)[1], 0)

    def tap(t, i):
        return taps[(t * STREAMS + i) * SUB : (t * STREAMS + i + 1) * SUB, :]

    def rows_of(t):
        return pl.ds(pl.multiple_of(t * SUB, SUB), SUB)

    def short(i, now, before, before2):
        return tap(0, i) * now + tap(1, i) * before + tap(2, i) * before2

    def mode(ref, m):
        return ref[m * SUB : (m + 1) * SUB, :]

    UN = 4
    zero = jnp.zeros((SUB, LN), F32)

    def state_one(rows, carry):
        k1, k2, v1, v2, *s = carry
        k0, v0 = xf[1, rows, :], xf[2, rows, :]
        value = short(1, k0, k1, k2) * short(2, v0, v1, v2)
        kv[rows, :] = value
        s = [mode(dec1, m) * s[m] + value for m in range(modes)]
        return (k0, k1, v0, v1, *s)

    def state_step(n, carry):
        for u in range(UN):
            carry = state_one(rows_of(n * UN + u), carry)
        return carry

    def at(i, t):
        return xf[i, t * SUB : (t + 1) * SUB, :]

    last = (at(1, 1), at(1, 0), at(2, 1), at(2, 0)) + (zero,) * modes
    for t in range(HALO, UN):
        last = state_one(rows_of(t), last)
    last = lax.fori_loop(
        1,
        T // UN,
        state_step,
        last,
    )
    for m in range(modes):
        st[m * SUB : (m + 1) * SUB, :] = last[4 + m]
    dec_a = jnp.exp(-rate[...] * float(T - 2))

    pl.semaphore_wait(barrier, len(partners))

    def halo_(): return rcopy(
        xf.at[:, pl.ds((T - HALO) * SUB, HALO * SUB), :],
        halo,
        halo_sem.at[0],
        halo_sem.at[1],
        {"seq": (seq + 1) % SEQ, "chan": chan},
    )
    halo_copy = halo_()
    halo_copy.start()

    def swap_(): return rcopy(w_hbm, w_all.at[x_lo, z], sw_sem.at[0], sw_sem.at[1], swap)

    swap_copy = swap_()
    @pl.when(jnp.logical_not(native))
    def _():
        swap_copy.start()

    up = dev((z + 1) % Z, g, chan)
    down = dev((z + Z - 1) % Z, g, chan)
    sibling = dev(z, x_hi * 2 + (1 - core), chan)
    HALF = Z // 2

    def w_chunk(k, zz, h):
        return w_all.at[k, zz, pl.ds(h * KH, KH), :]

    def ring_copy(flow, d, h):
        if flow == 0:
            zz, target, index = (z + Z - d + 1) % Z, up, 2 * d
        else:
            zz, target, index = (z + d - 1) % Z, down, 2 * d - 1
        if d == HALF:
            index = Z - 1
        ref = w_chunk(core, zz, h)
        return rcopy(ref, ref, w_ssem.at[flow, d - 1, h], w_rsem.at[index, h], target)

    def ring_halves(flow, d):
        return (0, 1) if d < HALF else ((0,) if flow == 0 else (1,))

    def rel(i):
        d = (i + 1) // 2
        return (z + Z + jnp.where(i % 2 == 1, d, -d)) % Z

    def sib_copy(i, h):
        ref = w_chunk(core, rel(i), h)
        return rcopy(ref, ref, sib_ssem.at[i, h], sib_rsem.at[i, h], sibling)

    def ring_first():
        for flow in range(2):
            ring_copy(flow, 1, 0).start()
        for h in range(2):
            sib_copy(0, h).start()

    def ring_second():
        for flow in range(2):
            ring_copy(flow, 1, 0).wait_send()
        for flow in range(2):
            ring_copy(flow, 1, 1).start()

    @pl.when(native)
    def _():
        load_w.wait()
        ring_first()
        ring_second()

    def pump(d, h):
        for flow in range(2):
            if h not in ring_halves(flow, d):
                continue
            ring_copy(flow, d, h).wait_recv()
            if d < HALF and h in ring_halves(flow, d + 1):
                ring_copy(flow, d + 1, h).start()
            i = Z - 1 if d == HALF else (2 * d if flow == 0 else 2 * d - 1)
            sib_copy(i, h).start()

    def other_start():
        @pl.when(jnp.logical_not(native))
        def _():
            swap_().wait_recv()
            ring_first()

    def pumps(cond, *steps):
        @pl.when(cond)
        def _():
            for d, h in steps:
                pump(d, h)

    other = jnp.logical_not(native)

    halo_copy.wait_recv()
    first = seq == 0

    def halo_tile(i, n):
        return jnp.where(first, 0.0, halo[i, n * SUB : (n + 1) * SUB, :])

    heads = []
    for t in range(HALO):
        pair = []
        for i in (1, 2):
            seen = [halo_tile(i, 0), halo_tile(i, 1), at(i, 0), at(i, 1)]
            pair.append(short(i, seen[t + 2], seen[t + 1], seen[t]))
        heads.append(pair[0] * pair[1])
        kv[t * SUB : (t + 1) * SUB, :] = heads[t]
    for m in range(modes):
        rows = slice(m * SUB, (m + 1) * SUB)
        st[rows, :] += dec_a[rows, :] * (mode(dec1, m) * heads[0] + heads[1])

    def quarter(j):
        return pl.ds(pl.multiple_of(j * QR, QR), QR)

    def p1_copy(r):
        peer = (g + r) % 4
        return rcopy(st.at[quarter(peer), :], p1.at[g], p1_sem.at[0, r - 1], p1_sem.at[1, r - 1], dev(z, peer, chan))

    for r in range(1, 4):
        p1_copy(r).start()
    p1[g] = st[quarter(g), :]

    def local_step(n, carry):
        q1, q2, *s = carry
        for u in range(UN):
            rows = rows_of(n * UN + u)
            q0, value = xf[0, rows, :], kv[rows, :]
            s = [mode(dec1, m) * s[m] + value for m in range(modes)]
            terms = [mode(coef, m) * s[m] for m in range(modes)]
            while len(terms) > 1:
                terms = [terms[2 * n_] + terms[2 * n_ + 1] for n_ in range(len(terms) // 2)]
            qf[rows, :] = short(0, q0, q1, q2)
            g0[rows, :] = terms[0] + skip_ref[...] * value
            q1, q2 = q0, q1
        return (q1, q2, *s)

    pumps(native, (1, 0))
    half_way = lax.fori_loop(0, T // UN // 2, local_step, (halo_tile(0, 1), halo_tile(0, 0)) + (zero,) * modes)
    for r in range(1, 4):
        p1_copy(r).wait_recv()
    my_t = dec_t[quarter(g), :]
    total = p1[0]
    for j in range(1, 4):
        total = total * my_t + p1[j]
    e_z[...] = total

    def p2_copy(zz, src_z):
        return rcopy(e_z, p2.at[src_z], p2_ssem.at[zz], p2_rsem.at[src_z], dev(zz, g, chan))

    lax.fori_loop(z + 1, Z, lambda zz, c: (p2_copy(zz, z).start(), c)[1], 0)

    other_start()
    pumps(native, (1, 1))
    lax.fori_loop(T // UN // 2, T // UN, local_step, half_way)
    pumps(native, (2, 0))

    my_g = dec_g[quarter(g), :]

    def carry_in(zz, c):
        p2_copy(zz, zz).wait_recv()
        return c * my_g + p2[zz]

    enter = lax.fori_loop(0, z, carry_in, jnp.zeros((QR, LN), F32))
    for j in range(4):
        p3_send[j] = enter
        enter = enter * my_t + p1[j]

    def p3_copy(r):
        peer = (g + r) % 4
        return rcopy(p3_send.at[peer], p3.at[quarter(g), :], p3_sem.at[0, r - 1], p3_sem.at[1, r - 1], dev(z, peer, chan))

    for r in range(1, 4):
        p3_copy(r).start()
    p3[quarter(g), :] = p3_send[g]

    @pl.when(other)
    def _():
        ring_second()

    pumps(native, (2, 1))
    pumps(other, (1, 0))
    for r in range(1, 4):
        p3_copy(r).wait_recv()

    def gate_step(n, w):
        w = list(w)
        for u in range(UN):
            rows = rows_of(n * UN + u)
            w = [mode(dec1, m) * w[m] for m in range(modes)]
            terms = w
            while len(terms) > 1:
                terms = [terms[2 * n_] + terms[2 * n_ + 1] for n_ in range(len(terms) // 2)]
            g0[rows, :] = qf[rows, :] * (g0[rows, :] + terms[0])
        return tuple(w)

    lax.fori_loop(0, T // UN, gate_step, tuple(mode(coef, m) * mode(p3, m) for m in range(modes)))

    def gather_rows(b, c):
        rows = pl.ds(pl.multiple_of(b * PAIR, PAIR), PAIR)
        for j in range(SUB):
            block = g0[pl.ds(b * PAIR * SUB + j, PAIR, stride=SUB), :]
            a_all[xx, rows, j * LN : (j + 1) * LN] = block.astype(BF16)
        return c

    lax.fori_loop(0, T // PAIR, gather_rows, 0)

    right, left = (xx + 1) % NX, (xx + NX - 1) % NX

    def a_copy(way, h, relay):
        rows = pl.ds(h * HT + (way * HT // 2 if relay else 0), HT // 2 if relay else HT)
        return rows, way + 2 * relay, x_dev(right if way == 0 else left)

    def a_out(way, h, relay=0):
        rows, slot, target = a_copy(way, h, relay)
        ref = a_all.at[(left if way == 0 else right) if relay else xx, rows, :]
        return rcopy(ref, ref, a_ssem.at[slot, h], a_rsem.at[slot, h], target)

    def a_in(way, h, relay=0):
        rows, slot, target = a_copy(way, h, relay)
        ref = a_all.at[(xx + 2) % NX if relay else (left if way == 0 else right), rows, :]
        return rcopy(ref, ref, a_ssem.at[slot, h], a_rsem.at[slot, h], target)

    def a_pass(h):
        for way in range(2):
            a_in(way, h).wait_recv()
            a_out(way, h, 1).start()

    def a_far(h):
        for way in range(2):
            a_in(way, h, 1).wait_recv()

    for way in range(2):
        a_out(way, 0).start()
    pumps(native, (3, 0))
    pumps(other, (1, 1))
    for way in range(2):
        a_out(way, 0).wait_send()
        a_out(way, 1).start()
    pumps(native, (3, 1))
    pumps(other, (2, 0))

    GROUPS = ((0, 3), (3, 5), (5, 7), (7, 8))

    def span(n):
        return pl.ds(GROUPS[n][0], GROUPS[n][1] - GROUPS[n][0])

    def y_next(way):
        return (y + 1) % Y if way == 0 else (y + Y - 1) % Y

    def r_copy(tb, n, way):
        return rcopy(
            c_send.at[tb, (y + 2) % Y, span(n), way],
            c_relay.at[way, tb, span(n)],
            r_ssem.at[way, tb, n],
            r_rsem.at[way, tb, n],
            dev(z, g, x_lo * Y + y_next(way)),
        )

    def c_copy(tb, n, way):
        return rcopy(
            c_send.at[tb, y_next(way), span(n)],
            c_recv.at[way, tb, span(n)],
            c_ssem.at[way, tb, n],
            c_rsem.at[way, tb, n],
            dev(z, g, x_lo * Y + y_next(way)),
        )

    def relay(tb, n):
        for way in range(2):
            r_copy(tb, n, way).wait_recv()
            peer = y_next(way)

            def step(i, c):
                mine = c_send[tb, peer, i, way].astype(F32)
                c_send[tb, peer, i, way] = (mine + c_relay[way, tb, i].astype(F32)).astype(BF16)
                return c

            lax.fori_loop(GROUPS[n][0], GROUPS[n][1], step, 0)
            c_copy(tb, n, way).start()

    def sib_wait(i):
        for h in range(2):
            ref = w_chunk(1 - core, rel(i), h)
            rcopy(ref, ref, sib_ssem.at[i, h], sib_rsem.at[i, h], sibling).wait_recv()

    def unit(tb, i, halves):
        zz = rel(i)
        rows = pl.ds(halves[0] * HT, len(halves) * HT)
        total = jnp.dot(a_all[2 * tb, rows, :], w_all[0, zz], preferred_element_type=F32)
        total += jnp.dot(a_all[2 * tb + 1, rows, :], w_all[1, zz], preferred_element_type=F32)
        value = total.astype(BF16)
        for at_, h in enumerate(halves):
            for n in range(Y):
                c_send[tb, n, i, h] = value[at_ * HT + n * QS : at_ * HT + (n + 1) * QS, :]

    def units(tb, n, halves, fresh=False):
        def step(i, c):
            if fresh:
                sib_wait(i)
            unit(tb, i, halves)
            return c

        lax.fori_loop(GROUPS[n][0], GROUPS[n][1], step, 0)
        for way in range(2):
            r_copy(tb, n, way).start()

    def o_copy(tb, i):
        zz = rel(i)
        return rcopy(
            o_send.at[tb, i],
            o_recv.at[xx, :, y],
            o_ssem.at[tb, i],
            o_rsem.at[here],
            dev(z, tb * 2 + core, zz),
        )

    def is_mine(tb, i):
        return jnp.logical_and(tb == x_hi, rel(i) == chan)

    def sum_group(tb, n):
        for way in range(2):
            c_copy(tb, n, way).wait_recv()

        def step(i, c):
            total = c_send[tb, y, i].astype(F32)
            for way in range(2):
                total += c_recv[way, tb, i].astype(F32)
            value = total.astype(BF16)

            @pl.when(is_mine(tb, i))
            def _():
                o_recv[xx, :, y] = value

            @pl.when(jnp.logical_not(is_mine(tb, i)))
            def _():
                o_send[tb, i] = value
                o_copy(tb, i).start()

            return c

        lax.fori_loop(GROUPS[n][0], GROUPS[n][1], step, 0)

    near, far = x_hi, 1 - x_hi
    whole = (0, 1)
    a_pass(0)
    pumps(other, (2, 1))
    a_pass(1)
    units(near, 0, whole, True)
    pumps(other, (3, 0))
    units(near, 1, whole, True)
    pumps(other, (3, 1))
    relay(near, 0)
    pumps(native, (4, 0), (4, 1))
    a_far(0)
    a_far(1)
    units(far, 0, whole)
    relay(near, 1)
    units(far, 1, whole)
    units(near, 2, whole, True)
    relay(far, 0)
    units(far, 2, whole)
    relay(far, 1)
    relay(near, 2)
    relay(far, 2)
    pumps(other, (4, 0), (4, 1))
    units(near, 3, whole, True)
    units(far, 3, whole)

    sum_group(near, 0)
    sum_group(near, 1)
    relay(near, 3)
    relay(far, 3)
    sum_group(far, 0)
    sum_group(far, 1)
    sum_group(near, 2)
    sum_group(far, 2)
    sum_group(near, 3)
    sum_group(far, 3)
    load_res.wait()
    load_emb.wait()

    def o_in(n):
        ref = o_recv.at[n // Y, :, n % Y]
        return rcopy(ref, ref, o_ssem.at[0, 0], o_rsem.at[n], sibling)

    def o_wait(n, c):
        @pl.when(n != here)
        def _():
            o_in(n).wait_recv()

        return c


    squares = jnp.zeros((T, LN), F32)
    logits = jnp.zeros((VB * CHAN, T), F32)
    for j in range(NX):
        lax.fori_loop(j * Y, (j + 1) * Y, o_wait, 0)
        cols = slice(j * NB, (j + 1) * NB)
        value = (res_v[:, cols].astype(F32) + o_recv[j].reshape(T, NB).astype(F32)).astype(BF16)
        bo_v[:, cols] = value
        wide = value.astype(F32)
        for n in range(NB // LN):
            part = wide[:, n * LN : (n + 1) * LN]
            squares += part * part
        scaled = (wide * gain_ref[:, cols]).astype(BF16)
        logits += lax.dot_general(emb_v[:, cols], scaled, (((1,), (1,)), ((), ())), preferred_element_type=F32)
    store_bo = pltpu.make_async_copy(bo_v, bo_hbm, loc_sem.at[6])
    store_bo.start()

    sums = jnp.sum(squares.T, axis=0, keepdims=True)
    high = sums.astype(BF16)
    low = (sums - high.astype(F32)).astype(BF16)
    row = lax.broadcasted_iota(jnp.int32, (PAIR, T), 0)
    extra = jnp.where(row == 0, high.astype(F32), jnp.where(row == 1, low.astype(F32), 0.0)).astype(BF16)
    for j in range(CHAN):
        l_send[j, :VB, :] = logits[j * VB : (j + 1) * VB, :].astype(BF16)
        l_send[j, VB:, :] = extra

    def l_copy(r):
        peer = (chan + r) % CHAN
        return rcopy(l_send.at[peer], l_recv.at[r - 1], l_sem.at[0, r - 1], l_sem.at[1, r - 1], dev(z, g, peer))

    for r in range(1, CHAN):
        l_copy(r).start()
    full = l_send[chan].astype(F32)
    for r in range(1, CHAN):
        l_copy(r).wait_recv()
        full += l_recv[r - 1].astype(F32)
    mean = (full[VB : VB + 1, :] + full[VB + 1 : VB + 2, :]) / float(C * CHAN)
    scaled_logits = full[:VB, :] * lax.rsqrt(mean + 1e-06)
    vocab = lax.broadcasted_iota(jnp.int32, (VB, T), 0) + chan * VB
    chosen = jnp.sum(jnp.where(vocab == ids_ref[...], scaled_logits, 0.0), axis=0, keepdims=True)
    top = jnp.max(scaled_logits, axis=0, keepdims=True)
    mass = jnp.sum(jnp.exp(scaled_logits - top), axis=0, keepdims=True)
    row = lax.broadcasted_iota(jnp.int32, (SUB, T), 0)
    s_send[...] = jnp.where(row == 0, top, jnp.where(row == 1, mass, jnp.where(row == 2, chosen, 0.0)))

    def s_copy(r):
        return rcopy(
            s_send, s_recv.at[r - 1], s_sem.at[0, r - 1], s_sem.at[1, r - 1], dev(z, g, (chan + r) % CHAN)
        )

    for r in range(1, CHAN):
        s_copy(r).start()
    best = top
    for r in range(1, CHAN):
        s_copy(r).wait_recv()
        best = jnp.maximum(best, s_recv[r - 1, 0:1, :])
    mass = mass * jnp.exp(top - best)
    for r in range(1, CHAN):
        mass += s_recv[r - 1, 1:2, :] * jnp.exp(s_recv[r - 1, 0:1, :] - best)
        chosen += s_recv[r - 1, 2:3, :]
    ll_ref[...] = chosen - best - jnp.log(mass)

    store_bo.wait()
    halo_copy.wait_send()

    @pl.when(jnp.logical_not(native))
    def _():
        swap_copy.wait_send()

    for flow in range(2):
        for d in range(1, HALF + 1):
            for h in ring_halves(flow, d):
                if (d, h) != (1, 0):
                    ring_copy(flow, d, h).wait_send()
    for i in range(Z):
        for h in range(2):
            sib_copy(i, h).wait_send()
    for r in range(1, 4):
        p1_copy(r).wait_send()
        p3_copy(r).wait_send()
    lax.fori_loop(z + 1, Z, lambda zz, c: (p2_copy(zz, z).wait_send(), c)[1], 0)
    for way in range(2):
        a_out(way, 1).wait_send()
        for h in range(2):
            a_out(way, h, 1).wait_send()
    for tb in range(2):
        for n in range(len(GROUPS)):
            for way in range(2):
                r_copy(tb, n, way).wait_send()
                c_copy(tb, n, way).wait_send()

    def o_done(n, c):
        tb, i = n // Z, n % Z

        @pl.when(jnp.logical_not(is_mine(tb, i)))
        def _():
            o_copy(tb, i).wait_send()

        return c

    lax.fori_loop(0, 2 * Z, o_done, 0)
    for r in range(1, CHAN):
        l_copy(r).wait_send()
        s_copy(r).wait_send()


def block(Z, Y, features, residual_in, short_filter, decay_rates, residues, skip_gain, out_weight, final_gain, embedding, next_ids):
    T, _, C = features.shape
    LN = C // SUB
    modes = decay_rates.shape[1]
    QR = modes // GROUP * SUB
    K, NB = out_weight.shape
    V = embedding.shape[0]
    CHAN = 2 * Y
    VB = V // CHAN
    QS = T // Y // 2
    DMA = pltpu.SemaphoreType.DMA
    hbm = pl.BlockSpec(memory_space=pl.ANY)
    vmem = pl.BlockSpec(memory_space=pltpu.VMEM)
    block_out, log_like = pl.pallas_call(
        functools.partial(kernel, Z, Y),
        out_shape=(jax.ShapeDtypeStruct((T, C), BF16), jax.ShapeDtypeStruct((1, T), F32)),
        in_specs=[hbm] * 10,
        out_specs=(hbm, vmem),
        scratch_shapes=[
            pltpu.VMEM((TAPS, STREAMS, C), F32),
            pltpu.VMEM((modes, C), F32),
            pltpu.VMEM((modes, C), F32),
            pltpu.VMEM((SUB, LN), F32),
            pltpu.VMEM((1, C), F32),
            pltpu.VMEM((1, T), jnp.int32),
            pltpu.VMEM((STREAMS, T, C), BF16),
            pltpu.VMEM((STREAMS, T * SUB, LN), F32),
            pltpu.VMEM((TAPS * STREAMS * SUB, LN), F32),
            pltpu.VMEM((modes * SUB, LN), F32),
            pltpu.VMEM((modes * SUB, LN), F32),
            pltpu.VMEM((modes * SUB, LN), F32),
            pltpu.VMEM((modes * SUB, LN), F32),
            pltpu.VMEM((modes * SUB, LN), F32),
            pltpu.VMEM((STREAMS, HALO * SUB, LN), F32),
            pltpu.VMEM((T * SUB, LN), F32),
            pltpu.VMEM((T * SUB, LN), F32),
            pltpu.VMEM((T * SUB, LN), F32),
            pltpu.VMEM((modes * SUB, LN), F32),
            pltpu.VMEM((GROUP, QR, LN), F32),
            pltpu.VMEM((QR, LN), F32),
            pltpu.VMEM((Z, QR, LN), F32),
            pltpu.VMEM((GROUP, QR, LN), F32),
            pltpu.VMEM((modes * SUB, LN), F32),
            pltpu.VMEM((2, Z, K, NB), BF16),
            pltpu.VMEM((4, T, C), BF16),
            pltpu.VMEM((2, Y, Z, 2, QS, NB), BF16),
            pltpu.VMEM((2, 2, Z, QS, NB), BF16),
            pltpu.VMEM((2, 2, Z, 2, QS, NB), BF16),
            pltpu.VMEM((2, Z, 2, QS, NB), BF16),
            pltpu.VMEM((4, 2, Y, QS, NB), BF16),
            pltpu.VMEM((T, C), BF16),
            pltpu.VMEM((V, C), BF16),
            pltpu.VMEM((T, C), BF16),
            pltpu.VMEM((CHAN, VB + PAIR, T), BF16),
            pltpu.VMEM((CHAN - 1, VB + PAIR, T), BF16),
            pltpu.VMEM((SUB, T), F32),
            pltpu.VMEM((CHAN - 1, SUB, T), F32),
            DMA((13,)),
            DMA((2,)),
            DMA((2, 3)),
            DMA((Z,)),
            DMA((Z,)),
            DMA((2, 3)),
            DMA((2,)),
            DMA((2, Z // 2, 2)),
            DMA((Z, 2)),
            DMA((Z, 2)),
            DMA((Z, 2)),
            DMA((4, 2)),
            DMA((4, 2)),
            DMA((2, 2, 4)),
            DMA((2, 2, 4)),
            DMA((2, 2, 4)),
            DMA((2, 2, 4)),
            DMA((2, Z)),
            DMA((4 * Y,)),
            DMA((2, CHAN - 1)),
            DMA((2, CHAN - 1)),
        ],
        compiler_params=pltpu.CompilerParams(
            collective_id=0, has_side_effects=True, vmem_limit_bytes=60 * 1024 * 1024
        ),
    )(
        features.transpose(1, 0, 2),
        residual_in,
        short_filter,
        decay_rates.T,
        residues.T,
        skip_gain.reshape(SUB, LN),
        out_weight,
        final_gain.reshape(1, C),
        embedding,
        next_ids.reshape(1, T),
    )
    return block_out, log_like.reshape(T)


def solution(mesh):
    return jax.shard_map(
        functools.partial(block, mesh.shape["seq"] // 4, mesh.shape["chan"] // 2),
        mesh=mesh,
        in_specs=(
            P("seq", None, "chan"),
            P("seq", "chan"),
            P(None, None, "chan"),
            P("chan", None),
            P("chan", None),
            P("chan"),
            P("chan", "seq"),
            P("chan"),
            P(None, "chan"),
            P("seq"),
        ),
        out_specs=(P("seq", "chan"), P("seq")),
        check_vma=False,
    )
```
